32 devices in a mesh: seq: 8 (over z, y), head: 4 (over x, core).
Axes of the slice: x: 2, y: 2, z: 4, core: 2. Of those that a mesh axis runs over, the one named last changes fastest.
Arguments:
- query: bfloat16 [4096, 4096], P('seq', 'head'), may hold values from -46 to 46
- key_rows: bfloat16 [4096, 256], P('seq'), may hold values from -6 to 6
- value_rows: bfloat16 [4096, 256], P('seq'), may hold values from -6 to 6
- grad_out: bfloat16 [4096, 4096], P('seq', 'head'), may hold values from -6 to 6
Outputs:
- grad_query: bfloat16 [4096, 4096], P('seq', 'head')
- grad_key: float32 [4096, 256], P('seq')
- grad_value: float32 [4096, 256], P('seq')
The draws below stay inside these ranges and needn't reach their ends.
All inputs are finite; a program needn't handle non-finite values.
Results may differ from the reference program's by a relative error of at most 0.0051.
Values may be sent and summed in bfloat16 or wider, within the bound.
No kernel may reach another device: no remote copies, remote signals or barrier semaphores. Data moves between devices by JAX's collectives and lax.ppermute only.
A program may use at most 128 MiB of HBM per device.

```python
import jax
import jax.numpy as jnp
from jax import lax

H = 16
DH = 256
WINDOW = 2048
TOK_DEV = 512
TOKENS = 4096


def shared_keys(key):
    base = jax.random.normal(jax.random.fold_in(key, 11), (TOKENS, DH), jnp.float32)
    return jnp.clip(base, -6.0, 6.0)


def draw_key_rows(key, part):
    return shared_keys(key).astype(jnp.bfloat16)


def draw_query(key, part):
    base = jax.random.normal(jax.random.fold_in(key, 21), (TOKENS, H * DH), jnp.float32)
    base = jnp.clip(base, -6.0, 6.0)
    return base.astype(jnp.bfloat16)


def level_of(key, shape, split, least, top_value):
    loudness, own = 1.0, jax.random.fold_in(key, 6)
    for dim, shards_of in split:
        draws = jnp.exp(jax.random.uniform(jax.random.fold_in(own, dim), (shards_of,), jnp.float32, least / len(split), top_value / len(split)))
        loudness = loudness * jnp.repeat(draws, shape[dim] // shards_of).reshape([-1 if axis == dim else 1 for axis in range(len(shape))])
    return loudness


def bell_draw(own_key, shape, scale, most, split=(), kind=jnp.bfloat16):
    array = scale * jax.random.normal(own_key, shape, jnp.float32)
    if split:
        array = array * level_of(own_key, shape, split, -0.22, 0.18)
    return jnp.clip(array, -most, most).astype(kind)


def setup_inputs(seed: int = 0) -> dict:
    key_list = jax.random.split(jax.random.key(seed), 5)
    query = draw_query(jax.random.fold_in(key_list[4], 71), 0)
    key_rows = draw_key_rows(jax.random.fold_in(key_list[4], 71), 0)
    value_rows = bell_draw(key_list[2], (TOKENS, DH), 1.0, 6.0, ((0, 8),))
    grad_out = bell_draw(key_list[3], (TOKENS, H * DH), 1.0, 6.0, ((0, 8), (1, 4)))
    return dict(query=query, key_rows=key_rows, value_rows=value_rows, grad_out=grad_out)


def reference(query, key_rows, value_rows, grad_out):
    total_rows = query.shape[0]
    head_dim = key_rows.shape[1]
    heads = query.shape[1] // head_dim
    score_scale = head_dim ** -0.5
    block_rows = min(512, TOK_DEV)
    queries = query.reshape(total_rows, heads, head_dim).astype(jnp.float32)
    grads = grad_out.reshape(total_rows, heads, head_dim).astype(jnp.float32)
    zero_rows = jnp.zeros((WINDOW, head_dim), jnp.float32)
    keys_padded = jnp.concatenate([zero_rows, key_rows.astype(jnp.float32)], axis=0)
    values_padded = jnp.concatenate([zero_rows, value_rows.astype(jnp.float32)], axis=0)
    row_ids = jnp.arange(block_rows, dtype=jnp.int32)
    col_ids = jnp.arange(WINDOW + block_rows, dtype=jnp.int32)
    high = lax.Precision.HIGHEST

    def step(carry, index_block):
        dk_acc, dv_acc = carry
        first_row = (index_block * block_rows).astype(jnp.int32)
        q_blk = lax.dynamic_slice_in_dim(queries, first_row, block_rows, 0)
        g_blk = lax.dynamic_slice_in_dim(grads, first_row, block_rows, 0)
        k_blk = lax.dynamic_slice_in_dim(keys_padded, first_row, WINDOW + block_rows, 0)
        v_blk = lax.dynamic_slice_in_dim(values_padded, first_row, WINDOW + block_rows, 0)
        key_pos = first_row - WINDOW + col_ids
        query_pos = first_row + row_ids
        gap_rows = query_pos[:, None] - key_pos[None, :]
        allowed = (gap_rows >= 0) & (gap_rows < WINDOW) & (key_pos >= 0)[None, :]
        scores = jnp.einsum('rhd,cd->hrc', q_blk, k_blk, precision=high) * score_scale
        scores = jnp.where(allowed[None], scores, -jnp.inf)
        row_max = jnp.max(scores, axis=-1, keepdims=True)
        expo = jnp.exp(scores - row_max)
        probs = expo / jnp.sum(expo, axis=-1, keepdims=True)
        probs_low = lax.optimization_barrier(probs.astype(jnp.bfloat16)).astype(jnp.float32)
        dv_blk = jnp.einsum('hrc,rhd->cd', probs_low, g_blk, precision=high)
        dprobs = jnp.einsum('rhd,cd->hrc', g_blk, v_blk, precision=high)
        delta = jnp.sum(probs * dprobs, axis=-1, keepdims=True)
        dscores = (probs * (dprobs - delta) * score_scale).astype(jnp.bfloat16)
        dscores = lax.optimization_barrier(dscores).astype(jnp.float32)
        dq_blk = jnp.einsum('hrc,cd->rhd', dscores, k_blk, precision=high).astype(jnp.bfloat16)
        dk_blk = jnp.einsum('hrc,rhd->cd', dscores, q_blk, precision=high)
        old_k = lax.dynamic_slice_in_dim(dk_acc, first_row, WINDOW + block_rows, 0)
        old_v = lax.dynamic_slice_in_dim(dv_acc, first_row, WINDOW + block_rows, 0)
        dk_acc = lax.dynamic_update_slice_in_dim(dk_acc, old_k + dk_blk, first_row, 0)
        dv_acc = lax.dynamic_update_slice_in_dim(dv_acc, old_v + dv_blk, first_row, 0)
        return (dk_acc, dv_acc), dq_blk.reshape(block_rows, heads * head_dim)

    start_acc = jnp.zeros((total_rows + WINDOW, head_dim), jnp.float32)
    blocks = jnp.arange(total_rows // block_rows, dtype=jnp.int32)
    (dk_acc, dv_acc), dq_all = lax.scan(step, (start_acc, start_acc), blocks)
    grad_query = dq_all.reshape(total_rows, heads * head_dim)
    return grad_query, dk_acc[WINDOW:], dv_acc[WINDOW:]
```

```python
import functools

import jax
import jax.numpy as jnp
from jax import lax
from jax.experimental import pallas as pl
from jax.experimental.pallas import tpu as pltpu
from jax.sharding import PartitionSpec as P

WINDOW = 2048
LOW = -1e30
VMEM_BYTES = 56 * 1024 * 1024


def along_seq(block, distance):
    count = lax.axis_size("seq")
    route = [(i, (i + distance) % count) for i in range(count)]
    return lax.ppermute(block, "seq", route)


def swap_heads(block, bit):
    route = [(i, i ^ bit) for i in range(lax.axis_size("head"))]
    return lax.ppermute(block, "head", route)


def dot_t(left, right):
    return lax.dot_general(
        left, right, (((1,), (1,)), ((), ())), preferred_element_type=jnp.float32
    )


def dot(left, right):
    return jnp.dot(left, right, preferred_element_type=jnp.float32)


def fold_rows(block, combine):
    rows = block.shape[0]
    while rows > 8:
        rows //= 2
        block = combine(block[:rows], block[rows:])
    return block


def lower_mask(half):
    keys = lax.broadcasted_iota(jnp.int32, (half, half), 0)
    queries = lax.broadcasted_iota(jnp.int32, (half, half), 1)
    return queries >= keys


def load_rows(own_ref, mine_refs, other_refs, ext, sem, core, half, reach):
    copies = []

    def copy(source, first):
        copies.append(
            pltpu.make_async_copy(source, ext.at[pl.ds(first, source.shape[0])], sem.at[len(copies)])
        )

    copy(own_ref, reach * 2 * half)
    for d in range(1, reach + 1):
        base = (reach - d) * 2 * half
        copy(mine_refs[d - 1], pl.multiple_of(base + core * half, half))
        copy(other_refs[d - 1], pl.multiple_of(base + (1 - core) * half, half))
    for each in copies:
        each.start()
    for each in copies:
        each.wait()


def corner_products(product, ext, rows, half, reach):
    far, own = 0, reach * 2 * half
    lo, hi = rows[:half], rows[half:]
    own_lo = product(ext[own : own + half], rows)
    own_hi = product(ext[own + half : own + 2 * half], hi)
    far_lo = product(ext[far : far + half], lo)
    far_hi = product(ext[far + half : far + 2 * half], rows)
    return own_lo, own_hi, far_lo, far_hi


def add_corner(corner, acc, rows, half, reach, mask):
    zero = jnp.zeros((half, half), corner.dtype)
    lo_lo, lo_hi = corner[:half, :half], corner[:half, half:]
    hi_lo, hi_hi = corner[half:, :half], corner[half:, half:]
    lo, hi = rows[:half], rows[half:]
    far, own = 0, reach * 2 * half
    acc[own : own + half] += dot(jnp.where(mask, lo_lo, zero), lo) + dot(lo_hi, hi)
    acc[own + half : own + 2 * half] += dot(jnp.where(mask, hi_hi, zero), hi)
    acc[far : far + half] += dot(jnp.where(mask, zero, lo_lo), lo)
    acc[far + half : far + 2 * half] += dot(hi_lo, lo) + dot(jnp.where(mask, zero, hi_hi), hi)


def split_out(acc, keep_ref, send_ref, core, half, reach):
    for d in range(reach + 1):
        base = (reach - d) * 2 * half
        keep_ref[d] = acc[pl.ds(pl.multiple_of(base + core * half, half), half), :]
        send_ref[d] = acc[pl.ds(pl.multiple_of(base + (1 - core) * half, half), half), :].astype(
            send_ref.dtype
        )


def probs_kernel(reach, scale, place, q_ref, g_ref, own_ref, *rest):
    mine_refs, other_refs, rest = rest[:reach], rest[reach : 2 * reach], rest[2 * reach :]
    e_ref, gs_ref, inv_ref, keep_ref, send_ref, ext, s_buf, acc, sem = rest
    head, heads = pl.program_id(0), pl.num_programs(0)
    rank, core = place[0], place[1]
    half = own_ref.shape[0] // 2
    full = 2 * half

    @pl.when(head == 0)
    def _():
        load_rows(own_ref, mine_refs, other_refs, ext, sem, core, half, reach)
        acc[...] = jnp.zeros_like(acc)

    mask = lower_mask(half)
    rows = q_ref[...] * jnp.asarray(scale, q_ref.dtype)
    far_bias = jnp.where(rank >= reach, 0.0, LOW).astype(jnp.float32)
    own_lo, own_hi, far_lo, far_hi = corner_products(dot_t, ext, rows, half, reach)
    s_buf[:half, :half] = jnp.where(mask, own_lo[:, :half], far_lo + far_bias)
    s_buf[:half, half:] = own_lo[:, half:]
    s_buf[half:full, :half] = far_hi[:, :half] + far_bias
    s_buf[half:full, half:] = jnp.where(mask, own_hi, far_hi[:, half:] + far_bias)
    top = fold_rows(s_buf[:full], jnp.maximum)
    for d in range(reach - 1, 0, -1):
        at = (reach - d) * full
        for first in (at, at + half):
            block = dot_t(ext[first : first + half], rows)
            s_buf[first : first + half] = block
            part = fold_rows(block, jnp.maximum)
            top = jnp.maximum(top, jnp.where(rank >= d, part, LOW))
    top = jnp.max(top, axis=0, keepdims=True)
    total = jnp.zeros((8, full), jnp.float32)
    for d in range(reach, 0, -1):
        at = (reach - d) * full
        level = top if d == reach else jnp.where(rank >= d, top, -LOW)
        for first in (at, at + half):
            expo = jnp.exp(s_buf[first : first + half] - level)
            total = total + fold_rows(expo, jnp.add)
            e_ref[0, first : first + half] = expo.astype(jnp.bfloat16)
    inv = 1.0 / jnp.sum(total, axis=0, keepdims=True)
    inv_rows = jnp.broadcast_to(inv, (8, full))
    inv_ref[0] = inv_rows
    scaled = (g_ref[...].astype(jnp.float32) * jnp.transpose(inv_rows)[:, :1]).astype(jnp.bfloat16)
    gs_ref[...] = scaled
    add_corner(e_ref[0, :full], acc, scaled, half, reach, mask)
    for d in range(reach - 1, 0, -1):
        at = (reach - d) * full
        acc[at : at + full] += dot(e_ref[0, at : at + full], scaled)

    @pl.when(head == heads - 1)
    def _():
        split_out(acc, keep_ref, send_ref, core, half, reach)


def dscores_kernel(reach, scale, place, q_ref, gs_ref, inv_ref, e_ref, own_ref, *rest):
    mine_refs, other_refs, rest = rest[:reach], rest[reach : 2 * reach], rest[2 * reach :]
    ds_ref, keep_ref, send_ref, ext, dp_buf, acc, sem = rest
    head, heads = pl.program_id(0), pl.num_programs(0)
    core = place[1]
    half = own_ref.shape[0] // 2
    full = 2 * half

    @pl.when(head == 0)
    def _():
        load_rows(own_ref, mine_refs, other_refs, ext, sem, core, half, reach)
        acc[...] = jnp.zeros_like(acc)

    mask = lower_mask(half)
    rows = gs_ref[...]
    own_lo, own_hi, far_lo, far_hi = corner_products(dot_t, ext, rows, half, reach)
    dp_buf[:half, :half] = jnp.where(mask, own_lo[:, :half], far_lo)
    dp_buf[:half, half:] = own_lo[:, half:]
    dp_buf[half:full, :half] = far_hi[:, :half]
    dp_buf[half:full, half:] = jnp.where(mask, own_hi, far_hi[:, half:])
    total = fold_rows(dp_buf[:full] * e_ref[0, :full].astype(jnp.float32), jnp.add)
    for first in range(full, reach * full, half):
        block = dot_t(ext[first : first + half], rows)
        dp_buf[first : first + half] = block
        total = total + fold_rows(
            block * e_ref[0, first : first + half].astype(jnp.float32), jnp.add
        )
    delta = jnp.sum(total, axis=0, keepdims=True) * inv_ref[0, :1]
    rows = q_ref[...] * jnp.asarray(scale, q_ref.dtype)
    for first in range(0, reach * full, half):
        block = e_ref[0, first : first + half].astype(jnp.float32) * (
            dp_buf[first : first + half] - delta
        )
        ds_ref[0, first : first + half] = block.astype(jnp.bfloat16)
    add_corner(ds_ref[0, :full], acc, rows, half, reach, mask)
    for first in range(full, reach * full, full):
        acc[first : first + full] += dot(ds_ref[0, first : first + full], rows)

    @pl.when(head == heads - 1)
    def _():
        split_out(acc, keep_ref, send_ref, core, half, reach)


def dquery_kernel(reach, scale, place, ds_ref, own_ref, *rest):
    mine_refs, other_refs, rest = rest[:reach], rest[reach : 2 * reach], rest[2 * reach :]
    dq_ref, ext, ext_t, sem = rest
    core = place[1]
    half = own_ref.shape[0] // 2
    full = 2 * half

    @pl.when(pl.program_id(0) == 0)
    def _():
        load_rows(own_ref, mine_refs, other_refs, ext, sem, core, half, reach)
        for first in range(0, (reach + 1) * full, half):
            ext_t[:, first : first + half] = jnp.transpose(ext[first : first + half])

    mask = lower_mask(half)
    zero = jnp.zeros((half, half), jnp.bfloat16)
    own = reach * full
    lo_lo, lo_hi = ds_ref[0, :half, :half], ds_ref[0, :half, half:]
    hi_lo, hi_hi = ds_ref[0, half:full, :half], ds_ref[0, half:full, half:]
    lo = (
        dot(ext_t[:, own : own + half], jnp.where(mask, lo_lo, zero))
        + dot(ext_t[:, :half], jnp.where(mask, zero, lo_lo))
        + dot(ext_t[:, half:full], hi_lo)
    )
    hi = (
        dot(ext_t[:, own : own + half], lo_hi)
        + dot(ext_t[:, own + half : own + full], jnp.where(mask, hi_hi, zero))
        + dot(ext_t[:, half:full], jnp.where(mask, zero, hi_hi))
    )
    total = dot(ext_t[:, full:own], ds_ref[0, full:own])
    lo = lo + total[:, :half]
    hi = hi + total[:, half:]
    dq_ref[:half] = jnp.transpose(lo * scale).astype(dq_ref.dtype)
    dq_ref[half:] = jnp.transpose(hi * scale).astype(dq_ref.dtype)


def gather_halo(rows, core, half, reach):
    piece = lax.dynamic_slice_in_dim(rows, core * half, half, 0)
    mine = [along_seq(piece, 1), along_seq(piece, 2)]
    for d in range(3, reach + 1):
        mine.append(along_seq(mine[d - 3], 2))
    other = [swap_heads(block, 1) for block in mine]
    return mine, other


def return_halo(keep, send, core, half, reach):
    total = keep + swap_heads(send, 1).astype(jnp.float32)
    parts = [total[d] for d in range(reach + 1)]
    for d in range(reach, 2, -1):
        back = along_seq(parts[d].astype(jnp.bfloat16), -2)
        parts[d - 2] = parts[d - 2] + back.astype(jnp.float32)
    own = parts[0]
    for d in (2, 1):
        own = own + along_seq(parts[d].astype(jnp.bfloat16), -d).astype(jnp.float32)
    bit = 2
    while bit < lax.axis_size("head"):
        low = own.astype(jnp.bfloat16)
        own = low.astype(jnp.float32) + swap_heads(low, bit).astype(jnp.float32)
        bit *= 2
    other = swap_heads(own, 1)
    first = jnp.where(core == 0, own, other)
    second = jnp.where(core == 0, other, own)
    return jnp.concatenate([first, second], axis=0)


def on_device(query, key_rows, value_rows, grad_out):
    tok_rows, head_dim = key_rows.shape
    heads = query.shape[1] // head_dim
    reach = WINDOW // tok_rows
    half = tok_rows // 2
    scale = head_dim ** (-0.5)
    core = lax.axis_index("head") % 2
    place = jnp.stack([lax.axis_index("seq"), core]).astype(jnp.int32)
    ext_rows = (reach + 1) * tok_rows
    span = reach * tok_rows

    smem = pl.BlockSpec(memory_space=pltpu.SMEM)
    hbm = pl.BlockSpec(memory_space=pl.ANY)
    by_head = pl.BlockSpec((tok_rows, head_dim), lambda h: (0, h))
    tiles = pl.BlockSpec((1, span, tok_rows), lambda h: (h, 0, 0))
    row = pl.BlockSpec((1, 8, tok_rows), lambda h: (h, 0, 0))
    whole = pl.BlockSpec((reach + 1, half, head_dim), lambda h: (0, 0, 0))
    tile_shape = jax.ShapeDtypeStruct((heads, span, tok_rows), jnp.bfloat16)
    keep_shape = jax.ShapeDtypeStruct((reach + 1, half, head_dim), jnp.float32)
    send_shape = jax.ShapeDtypeStruct((reach + 1, half, head_dim), jnp.bfloat16)
    ext = pltpu.VMEM((ext_rows, head_dim), jnp.bfloat16)
    acc = pltpu.VMEM((ext_rows, head_dim), jnp.float32)
    tile = pltpu.VMEM((span, tok_rows), jnp.float32)
    sems = pltpu.SemaphoreType.DMA((2 * reach + 1,))
    product = 2 * heads * tok_rows * (reach * tok_rows + half) * head_dim

    def call(body, name, products, **spec):
        return pl.pallas_call(
            functools.partial(body, reach, scale),
            grid=(heads,),
            compiler_params=pltpu.CompilerParams(vmem_limit_bytes=VMEM_BYTES),
            cost_estimate=pl.CostEstimate(
                flops=products * product, bytes_accessed=16 * 2**20, transcendentals=0
            ),
            name=name,
            **spec,
        )

    keys_mine, keys_other = gather_halo(key_rows, core, half, reach)
    values_mine, values_other = gather_halo(value_rows, core, half, reach)

    expo, grads, inv, dv_keep, dv_send = call(
        probs_kernel,
        "probs",
        2,
        in_specs=[smem, by_head, by_head] + [hbm] * (2 * reach + 1),
        out_specs=[tiles, by_head, row, whole, whole],
        out_shape=[
            tile_shape,
            jax.ShapeDtypeStruct(grad_out.shape, jnp.bfloat16),
            jax.ShapeDtypeStruct((heads, 8, tok_rows), jnp.float32),
            keep_shape,
            send_shape,
        ],
        scratch_shapes=[ext, tile, acc, sems],
    )(place, query, grad_out, key_rows, *keys_mine, *keys_other)

    dscores, dk_keep, dk_send = call(
        dscores_kernel,
        "dscores",
        2,
        in_specs=[smem, by_head, by_head, row, tiles] + [hbm] * (2 * reach + 1),
        out_specs=[tiles, whole, whole],
        out_shape=[tile_shape, keep_shape, send_shape],
        scratch_shapes=[ext, tile, acc, sems],
    )(place, query, grads, inv, expo, value_rows, *values_mine, *values_other)

    grad_value = return_halo(dv_keep, dv_send, core, half, reach)

    (grad_query,) = call(
        dquery_kernel,
        "dquery",
        1,
        in_specs=[smem, tiles] + [hbm] * (2 * reach + 1),
        out_specs=[by_head],
        out_shape=[jax.ShapeDtypeStruct(query.shape, query.dtype)],
        scratch_shapes=[ext, pltpu.VMEM((head_dim, ext_rows), jnp.bfloat16), sems],
    )(place, dscores, key_rows, *keys_mine, *keys_other)

    grad_key = return_halo(dk_keep, dk_send, core, half, reach)
    return grad_query, grad_key, grad_value


def solution(mesh):
    return jax.shard_map(
        on_device,
        mesh=mesh,
        in_specs=(P("seq", "head"), P("seq", None), P("seq", None), P("seq", "head")),
        out_specs=(P("seq", "head"), P("seq", None), P("seq", None)),
        check_vma=False,
    )
```

```python
import functools

import jax
import jax.numpy as jnp
from jax import lax
from jax.experimental import pallas as pl
from jax.experimental.pallas import tpu as pltpu
from jax.sharding import PartitionSpec as P

WINDOW = 2048
LOW = -1e30
VMEM_BYTES = 18 * 1024 * 1024


def along_seq(block, near, step):
    shards, group = lax.axis_size("seq"), lax.axis_size("head")
    route = []
    for shard in range(shards):
        for member in range(group):
            target = (shard + near + (member % 2) * step) % shards
            route.append((shard * group + member, target * group + member))
    return lax.ppermute(block, ("seq", "head"), route)


def swap_heads(block, bit):
    route = [(i, i ^ bit) for i in range(lax.axis_size("head"))]
    return lax.ppermute(block, "head", route)


def dot_t(left, right):
    return lax.dot_general(
        left, right, (((1,), (1,)), ((), ())), preferred_element_type=jnp.float32
    )


def dot(left, right):
    return jnp.dot(left, right, preferred_element_type=jnp.float32)


def fold_rows(block, total, combine):
    rows = total.shape[0]
    for first in range(0, block.shape[0], rows):
        total = combine(total, block[first : first + rows])
    return total


def lower_mask(half):
    keys = lax.broadcasted_iota(jnp.int32, (half, half), 0)
    queries = lax.broadcasted_iota(jnp.int32, (half, half), 1)
    return queries >= keys


def load_rows(own_ref, mine_refs, other_refs, ext, sem, core, full, reach):
    copies = [pltpu.make_async_copy(own_ref, ext.at[pl.ds(reach * full, full)], sem.at[0])]
    for j in range(reach // 2):
        first = pl.multiple_of((reach - 1 - 2 * j - core) * full, full)
        other = pl.multiple_of((reach - 2 - 2 * j + core) * full, full)
        copies.append(
            pltpu.make_async_copy(mine_refs[j], ext.at[pl.ds(first, full)], sem.at[2 * j + 1])
        )
        copies.append(
            pltpu.make_async_copy(other_refs[j], ext.at[pl.ds(other, full)], sem.at[2 * j + 2])
        )
    for each in copies:
        each.start()
    return copies


def unit_product(unit, ext, rows, half, reach, mask, far_bias=None):
    own = reach * 2 * half
    if unit >= 2:
        return dot_t(ext[unit * half : (unit + 1) * half], rows)
    if unit == 0:
        near = dot_t(ext[own : own + half], rows)
        far = dot_t(ext[:half], rows[:half])
        if far_bias is not None:
            far = far + far_bias
        return jnp.concatenate([jnp.where(mask, near[:, :half], far), near[:, half:]], axis=1)
    near = dot_t(ext[own + half : own + 2 * half], rows[half:])
    far = dot_t(ext[half : 2 * half], rows)
    if far_bias is not None:
        far = far + far_bias
    return jnp.concatenate([far[:, :half], jnp.where(mask, near, far[:, half:])], axis=1)


def unit_add(unit, tile, acc, rows, half, reach, mask):
    own = reach * 2 * half
    if unit >= 2:
        acc[unit * half : (unit + 1) * half] += dot(tile, rows)
        return
    left, right = tile[:, :half], tile[:, half:]
    zero = jnp.zeros_like(left)
    if unit == 0:
        both = jnp.concatenate([jnp.where(mask, left, zero), right], axis=1)
        acc[own : own + half] += dot(both, rows)
        acc[:half] += dot(jnp.where(mask, zero, left), rows[:half])
        return
    acc[own + half : own + 2 * half] += dot(jnp.where(mask, right, zero), rows[half:])
    both = jnp.concatenate([left, jnp.where(mask, zero, right)], axis=1)
    acc[half : 2 * half] += dot(both, rows)


def split_out(acc, own_ref, keep_ref, send_ref, core, full, reach):
    own_ref[...] = acc[reach * full :]
    for j in range(reach // 2):
        first = pl.multiple_of((reach - 1 - 2 * j - core) * full, full)
        other = pl.multiple_of((reach - 2 - 2 * j + core) * full, full)
        keep_ref[j] = acc[pl.ds(first, full), :]
        send_ref[j] = acc[pl.ds(other, full), :].astype(send_ref.dtype)


def probs_kernel(reach, scale, place, first_ref, q_ref, g_ref, own_ref, *rest):
    mine_refs, other_refs, rest = rest[: reach // 2], rest[reach // 2 : reach], rest[reach:]
    e_ref, gs_ref, inv_ref, down_ref, keep_ref, send_ref, ext, s_buf, peak_buf, acc, sem = rest
    step, steps = pl.program_id(0), pl.num_programs(0)
    rank, core = place[0], place[1]
    full = own_ref.shape[0]
    half = full // 2
    units = 2 * reach
    mask = lower_mask(half)
    far_bias = jnp.where(rank >= reach, 0.0, LOW).astype(jnp.float32)

    def score(unit, rows, peak):
        block = unit_product(unit, ext, rows, half, reach, mask, far_bias)
        s_buf[unit * half : (unit + 1) * half] = block
        part = fold_rows(block, jnp.full((16, full), LOW, jnp.float32), jnp.maximum)
        if unit >= 2:
            part = jnp.where(rank >= reach - unit // 2, part, LOW)
        return jnp.maximum(peak, part)

    lowest = jnp.full((16, full), LOW, jnp.float32)

    @pl.when(step == 0)
    def _():
        copies = load_rows(own_ref, mine_refs, other_refs, ext, sem, core, full, reach)
        acc[...] = jnp.zeros_like(acc)
        for each in copies:
            each.wait()
        rows = first_ref[...] * jnp.asarray(scale, q_ref.dtype)
        peak = lowest
        for unit in range(units):
            peak = score(unit, rows, peak)
        peak_buf[...] = peak

    rows = q_ref[...] * jnp.asarray(scale, q_ref.dtype)
    level = jnp.max(peak_buf[...], axis=0, keepdims=True)
    total = jnp.zeros((16, full), jnp.float32)
    peak = lowest
    for unit in range(units):
        d = reach - unit // 2
        at = slice(unit * half, (unit + 1) * half)
        high = level if unit < 2 else jnp.where(rank >= d, level, -LOW)
        expo = jnp.exp(s_buf[at] - high)
        total = fold_rows(expo, total, jnp.add)
        e_ref[step, at] = expo.astype(jnp.bfloat16)
        peak = score(unit, rows, peak)
    peak_buf[...] = peak
    inv = 1.0 / jnp.sum(total, axis=0, keepdims=True)
    inv_rows = jnp.broadcast_to(inv, (8, full))
    inv_ref[0] = inv_rows
    scaled = (g_ref[...].astype(jnp.float32) * jnp.transpose(inv_rows)[:, :1]).astype(jnp.bfloat16)
    gs_ref[...] = scaled
    for unit in range(units):
        at = slice(unit * half, (unit + 1) * half)
        unit_add(unit, e_ref[step, at], acc, scaled, half, reach, mask)

    @pl.when(step == steps - 1)
    def _():
        split_out(acc, down_ref, keep_ref, send_ref, core, full, reach)


def dscores_kernel(reach, scale, place, first_ref, first_inv, q_ref, gs_ref, *rest):
    inv_ref, e_ref, own_ref, rest = rest[0], rest[1], rest[2], rest[3:]
    mine_refs, other_refs, rest = rest[: reach // 2], rest[reach // 2 : reach], rest[reach:]
    ds_ref, down_ref, keep_ref, send_ref, ext, dp_buf, delta_buf, acc, sem = rest
    step, steps = pl.program_id(0), pl.num_programs(0)
    core = place[1]
    full = own_ref.shape[0]
    half = full // 2
    units = 2 * reach
    mask = lower_mask(half)

    def product(unit, grads, probs, total):
        at = slice(unit * half, (unit + 1) * half)
        block = unit_product(unit, ext, grads, half, reach, mask)
        dp_buf[at] = block
        return fold_rows(block * probs.astype(jnp.float32), total, jnp.add)

    def keep_delta(total, inv):
        delta_buf[...] = jnp.broadcast_to(
            jnp.sum(total, axis=0, keepdims=True) * inv, delta_buf.shape
        )

    nothing = jnp.zeros((16, full), jnp.float32)

    @pl.when(step == 0)
    def _():
        copies = load_rows(own_ref, mine_refs, other_refs, ext, sem, core, full, reach)
        acc[...] = jnp.zeros_like(acc)
        for each in copies:
            each.wait()
        grads = first_ref[...]
        total = nothing
        for unit in range(units):
            total = product(unit, grads, e_ref[0, unit * half : (unit + 1) * half], total)
        keep_delta(total, first_inv[0, :1])

    rows = q_ref[...] * jnp.asarray(scale, q_ref.dtype)
    grads = gs_ref[...]
    following = jnp.minimum(step + 1, steps - 1)
    delta = delta_buf[:1]
    total = nothing
    for unit in range(units):
        at = slice(unit * half, (unit + 1) * half)
        tile = (e_ref[step, at].astype(jnp.float32) * (dp_buf[at] - delta)).astype(jnp.bfloat16)
        ds_ref[step, at] = tile
        unit_add(unit, tile, acc, rows, half, reach, mask)
        total = product(unit, grads, e_ref[following, at], total)
    keep_delta(total, inv_ref[0, :1])

    @pl.when(step == steps - 1)
    def _():
        split_out(acc, down_ref, keep_ref, send_ref, core, full, reach)


def dot_first(left, right):
    return lax.dot_general(
        left, right, (((0,), (0,)), ((), ())), preferred_element_type=jnp.float32
    )


def dquery_kernel(reach, scale, place, ds_ref, own_ref, *rest):
    mine_refs, other_refs, rest = rest[: reach // 2], rest[reach // 2 : reach], rest[reach:]
    dq_ref, ext, sem = rest
    core = place[1]
    full = own_ref.shape[0]
    half = full // 2
    head = pl.program_id(0)

    @pl.when(pl.program_id(0) == 0)
    def _():
        copies = load_rows(own_ref, mine_refs, other_refs, ext, sem, core, full, reach)
        for each in copies:
            each.wait()

    mask = lower_mask(half)
    zero = jnp.zeros((half, half), jnp.bfloat16)
    own = reach * full
    lo_lo, lo_hi = ds_ref[head, :half, :half], ds_ref[head, :half, half:]
    hi_lo, hi_hi = ds_ref[head, half:full, :half], ds_ref[head, half:full, half:]
    lo = (
        dot_first(jnp.where(mask, lo_lo, zero), ext[own : own + half])
        + dot_first(jnp.where(mask, zero, lo_lo), ext[:half])
        + dot_first(hi_lo, ext[half:full])
    )
    hi = (
        dot_first(lo_hi, ext[own : own + half])
        + dot_first(jnp.where(mask, hi_hi, zero), ext[own + half : own + full])
        + dot_first(jnp.where(mask, zero, hi_hi), ext[half:full])
    )
    total = dot_first(ds_ref[head, full:own], ext[full:own])
    dq_ref[:half] = ((lo + total[:half]) * scale).astype(dq_ref.dtype)
    dq_ref[half:] = ((hi + total[half:]) * scale).astype(dq_ref.dtype)


def gather_relayed(rows, reach):
    mine = [along_seq(rows, 1, 1)]
    for _ in range(1, reach // 2):
        mine.append(along_seq(mine[-1], 2, 0))
    return mine, [swap_heads(block, 1) for block in mine]


def gather_direct(rows, reach):
    return [along_seq(rows, 2 * j + 1, 1) for j in range(reach // 2)]


def pair_sums(keep, send):
    return keep + swap_heads(send, 1).astype(jnp.float32)


def return_direct(parts):
    return [
        along_seq(parts[j].astype(jnp.bfloat16), -2 * j - 1, -1) for j in range(len(parts))
    ]


def sum_heads(down, core):
    half = down.shape[0] // 2
    mine = jnp.where(core == 0, down[:half], down[half:])
    other = jnp.where(core == 0, down[half:], down[:half])
    own = mine + swap_heads(other.astype(jnp.bfloat16), 1).astype(jnp.float32)
    bit = 2
    while bit < lax.axis_size("head"):
        low = own.astype(jnp.bfloat16)
        own = low.astype(jnp.float32) + swap_heads(low, bit).astype(jnp.float32)
        bit *= 2
    other = swap_heads(own, 1)
    first = jnp.where(core == 0, own, other)
    second = jnp.where(core == 0, other, own)
    return jnp.concatenate([first, second], axis=0)


def on_device(query, key_rows, value_rows, grad_out):
    tok_rows, head_dim = key_rows.shape
    heads = query.shape[1] // head_dim
    reach = WINDOW // tok_rows
    half = tok_rows // 2
    scale = head_dim ** (-0.5)
    core = lax.axis_index("head") % 2
    place = jnp.stack([lax.axis_index("seq"), core]).astype(jnp.int32)
    ext_rows = (reach + 1) * tok_rows
    span = reach * tok_rows

    def following(h):
        return jnp.minimum(h + 1, heads - 1)

    smem = pl.BlockSpec(memory_space=pltpu.SMEM)
    vmem = pl.BlockSpec(memory_space=pltpu.VMEM)
    halo = [pl.BlockSpec(memory_space=pl.ANY)] * (reach + 1)
    by_head = pl.BlockSpec((tok_rows, head_dim), lambda h: (0, h))
    by_head_next = pl.BlockSpec((tok_rows, head_dim), lambda h: (0, following(h)))
    by_head_first = pl.BlockSpec((tok_rows, head_dim), lambda h: (0, 0))
    row = pl.BlockSpec((1, 8, tok_rows), lambda h: (h, 0, 0))
    row_next = pl.BlockSpec((1, 8, tok_rows), lambda h: (following(h), 0, 0))
    row_first = pl.BlockSpec((1, 8, tok_rows), lambda h: (0, 0, 0))
    down = pl.BlockSpec((tok_rows, head_dim), lambda h: (0, 0))
    whole = pl.BlockSpec((reach // 2, tok_rows, head_dim), lambda h: (0, 0, 0))
    tile_shape = jax.ShapeDtypeStruct((heads, span, tok_rows), jnp.bfloat16)
    down_shape = jax.ShapeDtypeStruct((tok_rows, head_dim), jnp.float32)
    keep_shape = jax.ShapeDtypeStruct((reach // 2, tok_rows, head_dim), jnp.float32)
    send_shape = jax.ShapeDtypeStruct((reach // 2, tok_rows, head_dim), jnp.bfloat16)
    ext = pltpu.VMEM((ext_rows, head_dim), jnp.bfloat16)
    acc = pltpu.VMEM((ext_rows, head_dim), jnp.float32)
    tile = pltpu.VMEM((span, tok_rows), jnp.float32)
    wide = pltpu.VMEM((16, tok_rows), jnp.float32)
    sems = pltpu.SemaphoreType.DMA((reach + 1,))
    product = 2 * heads * tok_rows * (reach * tok_rows + half) * head_dim

    def call(body, name, products, **spec):
        return pl.pallas_call(
            functools.partial(body, reach, scale),
            grid=(heads,),
            compiler_params=pltpu.CompilerParams(vmem_limit_bytes=VMEM_BYTES),
            cost_estimate=pl.CostEstimate(
                flops=products * product, bytes_accessed=16 * 2**20, transcendentals=0
            ),
            name=name,
            **spec,
        )

    keys_mine, keys_other = gather_relayed(key_rows, reach)
    values_mine = gather_direct(value_rows, reach)

    expo, grads, inv, dv_down, dv_keep, dv_send = call(
        probs_kernel,
        "probs",
        2,
        in_specs=[smem, by_head_first, by_head_next, by_head] + halo,
        out_specs=[vmem, by_head, row, down, whole, whole],
        out_shape=[
            tile_shape,
            jax.ShapeDtypeStruct(grad_out.shape, jnp.bfloat16),
            jax.ShapeDtypeStruct((heads, 8, tok_rows), jnp.float32),
            down_shape,
            keep_shape,
            send_shape,
        ],
        scratch_shapes=[ext, tile, wide, acc, sems],
    )(place, query, query, grad_out, key_rows, *keys_mine, *keys_other)

    values_mine, expo, dv_keep, dv_send = lax.optimization_barrier(
        (values_mine, expo, dv_keep, dv_send)
    )
    values_other = [swap_heads(block, 1) for block in values_mine]
    dv_parts = pair_sums(dv_keep, dv_send)
    dv_parts, expo = lax.optimization_barrier((dv_parts, expo))
    dv_back = return_direct(dv_parts)

    dscores, dk_down, dk_keep, dk_send = call(
        dscores_kernel,
        "dscores",
        2,
        in_specs=[smem, by_head_first, row_first, by_head, by_head_next, row_next, vmem] + halo,
        out_specs=[vmem, down, whole, whole],
        out_shape=[tile_shape, down_shape, keep_shape, send_shape],
        scratch_shapes=[ext, tile, wide, acc, sems],
    )(place, grads, inv, query, grads, inv, expo, value_rows, *values_mine, *values_other)

    dv_back, dk_keep, dk_send = lax.optimization_barrier((dv_back, dk_keep, dk_send))
    for block in dv_back:
        dv_down = dv_down + block.astype(jnp.float32)
    dk_parts = pair_sums(dk_keep, dk_send)
    dk_parts, dscores = lax.optimization_barrier((dk_parts, dscores))
    dk_back = along_seq(dk_parts[-1].astype(jnp.bfloat16), -2, 0)

    (grad_query,) = call(
        dquery_kernel,
        "dquery",
        1,
        in_specs=[smem, vmem] + halo,
        out_specs=[by_head],
        out_shape=[jax.ShapeDtypeStruct(query.shape, query.dtype)],
        scratch_shapes=[ext, sems],
    )(place, dscores, key_rows, *keys_mine, *keys_other)

    dk_back, grad_query = lax.optimization_barrier((dk_back, grad_query))
    for j in range(reach // 2 - 2, -1, -1):
        piece = (dk_parts[j] + dk_back.astype(jnp.float32)).astype(jnp.bfloat16)
        dk_back = along_seq(piece, -2, 0) if j else along_seq(piece, -1, -1)
    grad_value = sum_heads(dv_down, core)
    grad_key = sum_heads(dk_down + dk_back.astype(jnp.float32), core)
    return grad_query, grad_key, grad_value


def solution(mesh):
    return jax.shard_map(
        on_device,
        mesh=mesh,
        in_specs=(P("seq", "head"), P("seq", None), P("seq", None), P("seq", "head")),
        out_specs=(P("seq", "head"), P("seq", None), P("seq", None)),
        check_vma=False,
    )
```

```python
import functools

import jax
import jax.numpy as jnp
from jax import lax
from jax.experimental import pallas as pl
from jax.experimental.pallas import tpu as pltpu
from jax.sharding import PartitionSpec as P

WINDOW = 2048
LOW = -1e30
VMEM_BYTES = 18 * 1024 * 1024


def along_seq(block, near, step):
    shards, group = lax.axis_size("seq"), lax.axis_size("head")
    route = []
    for shard in range(shards):
        for member in range(group):
            target = (shard + near + (member % 2) * step) % shards
            route.append((shard * group + member, target * group + member))
    return lax.ppermute(block, ("seq", "head"), route)


def swap_heads(block, bit):
    route = [(i, i ^ bit) for i in range(lax.axis_size("head"))]
    return lax.ppermute(block, "head", route)


def dot_t(left, right):
    return lax.dot_general(
        left, right, (((1,), (1,)), ((), ())), preferred_element_type=jnp.float32
    )


def dot(left, right):
    return jnp.dot(left, right, preferred_element_type=jnp.float32)


def fold_rows(block, total, combine):
    rows = total.shape[0]
    for first in range(0, block.shape[0], rows):
        total = combine(total, block[first : first + rows])
    return total


def lower_mask(half):
    keys = lax.broadcasted_iota(jnp.int32, (half, half), 0)
    queries = lax.broadcasted_iota(jnp.int32, (half, half), 1)
    return queries >= keys


def load_rows(own_ref, mine_refs, other_refs, ext, sem, core, full, reach):
    copies = [pltpu.make_async_copy(own_ref, ext.at[pl.ds(reach * full, full)], sem.at[0])]
    for j in range(reach // 2):
        first = pl.multiple_of((reach - 1 - 2 * j - core) * full, full)
        other = pl.multiple_of((reach - 2 - 2 * j + core) * full, full)
        copies.append(
            pltpu.make_async_copy(mine_refs[j], ext.at[pl.ds(first, full)], sem.at[2 * j + 1])
        )
        copies.append(
            pltpu.make_async_copy(other_refs[j], ext.at[pl.ds(other, full)], sem.at[2 * j + 2])
        )
    for each in copies:
        each.start()
    return copies


def unit_product(unit, ext, rows, half, reach, mask, far_bias=None):
    own = reach * 2 * half
    if unit >= 2:
        return dot_t(ext[unit * half : (unit + 1) * half], rows)
    if unit == 0:
        near = dot_t(ext[own : own + half], rows)
        far = dot_t(ext[:half], rows[:half])
        if far_bias is not None:
            far = far + far_bias
        return jnp.concatenate([jnp.where(mask, near[:, :half], far), near[:, half:]], axis=1)
    near = dot_t(ext[own + half : own + 2 * half], rows[half:])
    far = dot_t(ext[half : 2 * half], rows)
    if far_bias is not None:
        far = far + far_bias
    return jnp.concatenate([far[:, :half], jnp.where(mask, near, far[:, half:])], axis=1)


def unit_add(unit, tile, acc, rows, half, reach, mask):
    own = reach * 2 * half
    if unit >= 2:
        acc[unit * half : (unit + 1) * half] += dot(tile, rows)
        return
    left, right = tile[:, :half], tile[:, half:]
    zero = jnp.zeros_like(left)
    if unit == 0:
        both = jnp.concatenate([jnp.where(mask, left, zero), right], axis=1)
        acc[own : own + half] += dot(both, rows)
        acc[:half] += dot(jnp.where(mask, zero, left), rows[:half])
        return
    acc[own + half : own + 2 * half] += dot(jnp.where(mask, right, zero), rows[half:])
    both = jnp.concatenate([left, jnp.where(mask, zero, right)], axis=1)
    acc[half : 2 * half] += dot(both, rows)


def split_out(acc, own_ref, keep_ref, send_ref, core, full, reach):
    own_ref[...] = acc[reach * full :]
    for j in range(reach // 2):
        first = pl.multiple_of((reach - 1 - 2 * j - core) * full, full)
        other = pl.multiple_of((reach - 2 - 2 * j + core) * full, full)
        keep_ref[j] = acc[pl.ds(first, full), :]
        send_ref[j] = acc[pl.ds(other, full), :].astype(send_ref.dtype)


def probs_kernel(reach, scale, place, first_ref, q_ref, g_ref, own_ref, *rest):
    mine_refs, other_refs, rest = rest[: reach // 2], rest[reach // 2 : reach], rest[reach:]
    e_ref, gs_ref, inv_ref, down_ref, keep_ref, send_ref, ext, s_buf, peak_buf, acc, sem = rest
    step, steps = pl.program_id(0), pl.num_programs(0)
    rank, core = place[0], place[1]
    full = own_ref.shape[0]
    half = full // 2
    units = 2 * reach
    mask = lower_mask(half)
    far_bias = jnp.where(rank >= reach, 0.0, LOW).astype(jnp.float32)

    def score(unit, rows, peak):
        block = unit_product(unit, ext, rows, half, reach, mask, far_bias)
        s_buf[unit * half : (unit + 1) * half] = block
        part = fold_rows(block, jnp.full((16, full), LOW, jnp.float32), jnp.maximum)
        if unit >= 2:
            part = jnp.where(rank >= reach - unit // 2, part, LOW)
        return jnp.maximum(peak, part)

    lowest = jnp.full((16, full), LOW, jnp.float32)

    @pl.when(step == 0)
    def _():
        copies = load_rows(own_ref, mine_refs, other_refs, ext, sem, core, full, reach)
        acc[...] = jnp.zeros_like(acc)
        for each in copies:
            each.wait()
        rows = first_ref[...] * jnp.asarray(scale, q_ref.dtype)
        peak = lowest
        for unit in range(units):
            peak = score(unit, rows, peak)
        peak_buf[...] = peak

    rows = q_ref[...] * jnp.asarray(scale, q_ref.dtype)
    level = jnp.max(peak_buf[...], axis=0, keepdims=True)
    total = jnp.zeros((16, full), jnp.float32)
    peak = lowest
    for unit in range(units):
        d = reach - unit // 2
        at = slice(unit * half, (unit + 1) * half)
        high = level if unit < 2 else jnp.where(rank >= d, level, -LOW)
        expo = jnp.exp(s_buf[at] - high)
        total = fold_rows(expo, total, jnp.add)
        e_ref[step, at] = expo.astype(jnp.bfloat16)
        peak = score(unit, rows, peak)
    peak_buf[...] = peak
    inv = 1.0 / jnp.sum(total, axis=0, keepdims=True)
    inv_rows = jnp.broadcast_to(inv, (8, full))
    inv_ref[0] = inv_rows
    scaled = (g_ref[...].astype(jnp.float32) * jnp.transpose(inv_rows)[:, :1]).astype(jnp.bfloat16)
    gs_ref[...] = scaled
    for unit in range(units):
        at = slice(unit * half, (unit + 1) * half)
        unit_add(unit, e_ref[step, at], acc, scaled, half, reach, mask)

    @pl.when(step == steps - 1)
    def _():
        split_out(acc, down_ref, keep_ref, send_ref, core, full, reach)


def dscores_kernel(reach, scale, place, first_ref, first_inv, q_ref, gs_ref, *rest):
    inv_ref, e_ref, own_ref, rest = rest[0], rest[1], rest[2], rest[3:]
    mine_refs, other_refs, rest = rest[: reach // 2], rest[reach // 2 : reach], rest[reach:]
    ds_ref, down_ref, keep_ref, send_ref, ext, dp_buf, delta_buf, acc, sem = rest
    step, steps = pl.program_id(0), pl.num_programs(0)
    core = place[1]
    full = own_ref.shape[0]
    half = full // 2
    units = 2 * reach
    mask = lower_mask(half)

    def product(unit, grads, probs, total):
        at = slice(unit * half, (unit + 1) * half)
        block = unit_product(unit, ext, grads, half, reach, mask)
        dp_buf[at] = block
        return fold_rows(block * probs.astype(jnp.float32), total, jnp.add)

    def keep_delta(total, inv):
        delta_buf[...] = jnp.broadcast_to(
            jnp.sum(total, axis=0, keepdims=True) * inv, delta_buf.shape
        )

    nothing = jnp.zeros((16, full), jnp.float32)

    @pl.when(step == 0)
    def _():
        copies = load_rows(own_ref, mine_refs, other_refs, ext, sem, core, full, reach)
        acc[...] = jnp.zeros_like(acc)
        for each in copies:
            each.wait()
        grads = first_ref[...]
        total = nothing
        for unit in range(units):
            total = product(unit, grads, e_ref[0, unit * half : (unit + 1) * half], total)
        keep_delta(total, first_inv[0, :1])

    rows = q_ref[...] * jnp.asarray(scale, q_ref.dtype)
    grads = gs_ref[...]
    following = jnp.minimum(step + 1, steps - 1)
    delta = delta_buf[:1]
    total = nothing
    for unit in range(units):
        at = slice(unit * half, (unit + 1) * half)
        tile = (e_ref[step, at].astype(jnp.float32) * (dp_buf[at] - delta)).astype(jnp.bfloat16)
        ds_ref[step, at] = tile
        unit_add(unit, tile, acc, rows, half, reach, mask)
        total = product(unit, grads, e_ref[following, at], total)
    keep_delta(total, inv_ref[0, :1])

    @pl.when(step == steps - 1)
    def _():
        split_out(acc, down_ref, keep_ref, send_ref, core, full, reach)


def dot_first(left, right):
    return lax.dot_general(
        left, right, (((0,), (0,)), ((), ())), preferred_element_type=jnp.float32
    )


def dquery_kernel(reach, scale, place, ds_ref, own_ref, *rest):
    mine_refs, other_refs, rest = rest[: reach // 2], rest[reach // 2 : reach], rest[reach:]
    dq_ref, ext, sem = rest
    core = place[1]
    full = own_ref.shape[0]
    half = full // 2
    head = pl.program_id(0)

    @pl.when(pl.program_id(0) == 0)
    def _():
        copies = load_rows(own_ref, mine_refs, other_refs, ext, sem, core, full, reach)
        for each in copies:
            each.wait()

    mask = lower_mask(half)
    zero = jnp.zeros((half, half), jnp.bfloat16)
    own = reach * full
    lo_lo, lo_hi = ds_ref[head, :half, :half], ds_ref[head, :half, half:]
    hi_lo, hi_hi = ds_ref[head, half:full, :half], ds_ref[head, half:full, half:]
    lo = (
        dot_first(jnp.where(mask, lo_lo, zero), ext[own : own + half])
        + dot_first(jnp.where(mask, zero, lo_lo), ext[:half])
        + dot_first(hi_lo, ext[half:full])
    )
    hi = (
        dot_first(lo_hi, ext[own : own + half])
        + dot_first(jnp.where(mask, hi_hi, zero), ext[own + half : own + full])
        + dot_first(jnp.where(mask, zero, hi_hi), ext[half:full])
    )
    total = dot_first(ds_ref[head, full:own], ext[full:own])
    dq_ref[:half] = ((lo + total[:half]) * scale).astype(dq_ref.dtype)
    dq_ref[half:] = ((hi + total[half:]) * scale).astype(dq_ref.dtype)


def gather_relayed(rows, reach, scalars):
    first, scalars = lax.optimization_barrier((along_seq(rows, 1, 1), scalars))
    mine = [first]
    for _ in range(1, reach // 2):
        mine.append(along_seq(mine[-1], 2, 0))
    return mine, [swap_heads(block, 1) for block in mine], scalars


def gather_direct(rows, reach):
    return [along_seq(rows, 2 * j + 1, 1) for j in range(reach // 2)]


def pair_sums(keep, send):
    return keep + swap_heads(send, 1).astype(jnp.float32)


def relay_on(parts, arrived, reach):
    for j in range(reach // 2 - 2, -1, -1):
        piece = (parts[j] + arrived.astype(jnp.float32)).astype(jnp.bfloat16)
        arrived = along_seq(piece, -2, 0) if j else along_seq(piece, -1, -1)
    return arrived


def sum_heads(down, low_core):
    half = down.shape[0] // 2
    mine = jnp.where(low_core, down[:half], down[half:])
    other = jnp.where(low_core, down[half:], down[:half])
    own = mine + swap_heads(other.astype(jnp.bfloat16), 1).astype(jnp.float32)
    bit = 2
    while bit < lax.axis_size("head"):
        low = own.astype(jnp.bfloat16)
        own = low.astype(jnp.float32) + swap_heads(low, bit).astype(jnp.float32)
        bit *= 2
    other = swap_heads(own, 1)
    first = jnp.where(low_core, own, other)
    second = jnp.where(low_core, other, own)
    return jnp.concatenate([first, second], axis=0)


def on_device(query, key_rows, value_rows, grad_out):
    tok_rows, head_dim = key_rows.shape
    heads = query.shape[1] // head_dim
    reach = WINDOW // tok_rows
    half = tok_rows // 2
    scale = head_dim ** (-0.5)
    core = lax.axis_index("head") % 2
    place = jnp.stack([lax.axis_index("seq"), core]).astype(jnp.int32)
    ext_rows = (reach + 1) * tok_rows
    span = reach * tok_rows

    def following(h):
        return jnp.minimum(h + 1, heads - 1)

    smem = pl.BlockSpec(memory_space=pltpu.SMEM)
    vmem = pl.BlockSpec(memory_space=pltpu.VMEM)
    halo = [pl.BlockSpec(memory_space=pl.ANY)] * (reach + 1)
    by_head = pl.BlockSpec((tok_rows, head_dim), lambda h: (0, h))
    by_head_next = pl.BlockSpec((tok_rows, head_dim), lambda h: (0, following(h)))
    by_head_first = pl.BlockSpec((tok_rows, head_dim), lambda h: (0, 0))
    row = pl.BlockSpec((1, 8, tok_rows), lambda h: (h, 0, 0))
    row_next = pl.BlockSpec((1, 8, tok_rows), lambda h: (following(h), 0, 0))
    row_first = pl.BlockSpec((1, 8, tok_rows), lambda h: (0, 0, 0))
    down = pl.BlockSpec((tok_rows, head_dim), lambda h: (0, 0))
    whole = pl.BlockSpec((reach // 2, tok_rows, head_dim), lambda h: (0, 0, 0))
    tile_shape = jax.ShapeDtypeStruct((heads, span, tok_rows), jnp.bfloat16)
    down_shape = jax.ShapeDtypeStruct((tok_rows, head_dim), jnp.float32)
    keep_shape = jax.ShapeDtypeStruct((reach // 2, tok_rows, head_dim), jnp.float32)
    send_shape = jax.ShapeDtypeStruct((reach // 2, tok_rows, head_dim), jnp.bfloat16)
    ext = pltpu.VMEM((ext_rows, head_dim), jnp.bfloat16)
    acc = pltpu.VMEM((ext_rows, head_dim), jnp.float32)
    tile = pltpu.VMEM((span, tok_rows), jnp.float32)
    wide = pltpu.VMEM((16, tok_rows), jnp.float32)
    sems = pltpu.SemaphoreType.DMA((reach + 1,))
    product = 2 * heads * tok_rows * (reach * tok_rows + half) * head_dim

    def call(body, name, products, **spec):
        return pl.pallas_call(
            functools.partial(body, reach, scale),
            grid=(heads,),
            compiler_params=pltpu.CompilerParams(vmem_limit_bytes=VMEM_BYTES),
            cost_estimate=pl.CostEstimate(
                flops=products * product, bytes_accessed=16 * 2**20, transcendentals=0
            ),
            name=name,
            **spec,
        )

    keys_mine, keys_other, (place, low_core) = gather_relayed(key_rows, reach, (place, core == 0))
    values_mine = gather_direct(value_rows, reach)

    expo, grads, inv, dv_down, dv_keep, dv_send = call(
        probs_kernel,
        "probs",
        2,
        in_specs=[smem, by_head_first, by_head_next, by_head] + halo,
        out_specs=[vmem, by_head, row, down, whole, whole],
        out_shape=[
            tile_shape,
            jax.ShapeDtypeStruct(grad_out.shape, jnp.bfloat16),
            jax.ShapeDtypeStruct((heads, 8, tok_rows), jnp.float32),
            down_shape,
            keep_shape,
            send_shape,
        ],
        scratch_shapes=[ext, tile, wide, acc, sems],
    )(place, query, query, grad_out, key_rows, *keys_mine, *keys_other)

    values_mine, expo, dv_keep, dv_send = lax.optimization_barrier(
        (values_mine, expo, dv_keep, dv_send)
    )
    values_other = [swap_heads(block, 1) for block in values_mine]
    dv_parts = pair_sums(dv_keep, dv_send)
    dv_parts, expo = lax.optimization_barrier((dv_parts, expo))
    dv_back = along_seq(dv_parts[-1].astype(jnp.bfloat16), -2, 0)

    dscores, dk_down, dk_keep, dk_send = call(
        dscores_kernel,
        "dscores",
        2,
        in_specs=[smem, by_head_first, row_first, by_head, by_head_next, row_next, vmem] + halo,
        out_specs=[vmem, down, whole, whole],
        out_shape=[tile_shape, down_shape, keep_shape, send_shape],
        scratch_shapes=[ext, tile, wide, acc, sems],
    )(place, grads, inv, query, grads, inv, expo, value_rows, *values_mine, *values_other)

    dv_back, dk_keep, dk_send = lax.optimization_barrier((dv_back, dk_keep, dk_send))
    dk_parts = pair_sums(dk_keep, dk_send)
    dk_parts, dscores = lax.optimization_barrier((dk_parts, dscores))
    dk_back = along_seq(dk_parts[-1].astype(jnp.bfloat16), -2, 0)
    dv_back = relay_on(dv_parts, dv_back, reach)

    (grad_query,) = call(
        dquery_kernel,
        "dquery",
        1,
        in_specs=[smem, vmem] + halo,
        out_specs=[by_head],
        out_shape=[jax.ShapeDtypeStruct(query.shape, query.dtype)],
        scratch_shapes=[ext, sems],
    )(place, dscores, key_rows, *keys_mine, *keys_other)

    dk_back, dv_back, grad_query = lax.optimization_barrier((dk_back, dv_back, grad_query))
    dk_back = relay_on(dk_parts, dk_back, reach)
    grad_value = sum_heads(dv_down + dv_back.astype(jnp.float32), low_core)
    grad_key = sum_heads(dk_down + dk_back.astype(jnp.float32), low_core)
    return grad_query, grad_key, grad_value


def solution(mesh):
    return jax.shard_map(
        on_device,
        mesh=mesh,
        in_specs=(P("seq", "head"), P("seq", None), P("seq", None), P("seq", "head")),
        out_specs=(P("seq", "head"), P("seq", None), P("seq", None)),
        check_vma=False,
    )
```

```python
import functools

import jax
import jax.numpy as jnp
from jax import lax
from jax.experimental import pallas as pl
from jax.experimental.pallas import tpu as pltpu
from jax.sharding import PartitionSpec as P

WINDOW = 2048
LOW = -1e30
VMEM_BYTES = 18 * 1024 * 1024


def along_seq(block, near, step=0):
    shards, group = lax.axis_size("seq"), lax.axis_size("head")
    route = []
    for shard in range(shards):
        for member in range(group):
            target = (shard + near + (member % 2) * step) % shards
            route.append((shard * group + member, target * group + member))
    return lax.ppermute(block, ("seq", "head"), route)


def swap_heads(block, bit):
    route = [(i, i ^ bit) for i in range(lax.axis_size("head"))]
    return lax.ppermute(block, "head", route)


def dot_t(left, right):
    return lax.dot_general(
        left, right, (((1,), (1,)), ((), ())), preferred_element_type=jnp.float32
    )


def dot(left, right):
    return jnp.dot(left, right, preferred_element_type=jnp.float32)


def fold_rows(block, total, combine):
    rows = total.shape[0]
    for first in range(0, block.shape[0], rows):
        total = combine(total, block[first : first + rows])
    return total


def lower_mask(half):
    keys = lax.broadcasted_iota(jnp.int32, (half, half), 0)
    queries = lax.broadcasted_iota(jnp.int32, (half, half), 1)
    return queries >= keys


def load_rows(own_ref, mine_refs, other_refs, ext, sem, core, full, reach):
    copies = [pltpu.make_async_copy(own_ref, ext.at[pl.ds(reach * full, full)], sem.at[0])]
    for j in range(reach // 2):
        first = pl.multiple_of((reach - 1 - 2 * j - core) * full, full)
        other = pl.multiple_of((reach - 2 - 2 * j + core) * full, full)
        copies.append(
            pltpu.make_async_copy(mine_refs[j], ext.at[pl.ds(first, full)], sem.at[2 * j + 1])
        )
        copies.append(
            pltpu.make_async_copy(other_refs[j], ext.at[pl.ds(other, full)], sem.at[2 * j + 2])
        )
    for each in copies:
        each.start()
    return copies


def unit_product(unit, ext, rows, half, reach, mask, far_bias=None):
    own = reach * 2 * half
    if unit >= 2:
        return dot_t(ext[unit * half : (unit + 1) * half], rows)
    if unit == 0:
        near = dot_t(ext[own : own + half], rows)
        far = dot_t(ext[:half], rows[:half])
        if far_bias is not None:
            far = far + far_bias
        return jnp.concatenate([jnp.where(mask, near[:, :half], far), near[:, half:]], axis=1)
    near = dot_t(ext[own + half : own + 2 * half], rows[half:])
    far = dot_t(ext[half : 2 * half], rows)
    if far_bias is not None:
        far = far + far_bias
    return jnp.concatenate([far[:, :half], jnp.where(mask, near, far[:, half:])], axis=1)


def unit_add(unit, tile, acc, rows, half, reach, mask):
    own = reach * 2 * half
    if unit >= 2:
        acc[unit * half : (unit + 1) * half] += dot(tile, rows)
        return
    left, right = tile[:, :half], tile[:, half:]
    zero = jnp.zeros_like(left)
    if unit == 0:
        both = jnp.concatenate([jnp.where(mask, left, zero), right], axis=1)
        acc[own : own + half] += dot(both, rows)
        acc[:half] += dot(jnp.where(mask, zero, left), rows[:half])
        return
    acc[own + half : own + 2 * half] += dot(jnp.where(mask, right, zero), rows[half:])
    both = jnp.concatenate([left, jnp.where(mask, zero, right)], axis=1)
    acc[half : 2 * half] += dot(both, rows)


def split_out(acc, down_ref, keep_ref, send_ref, core, full, reach):
    down_ref[...] = acc[reach * full :]
    for j in range(reach // 2):
        first = pl.multiple_of((reach - 1 - 2 * j - core) * full, full)
        other = pl.multiple_of((reach - 2 - 2 * j + core) * full, full)
        keep_ref[j] = acc[pl.ds(first, full), :]
        send_ref[j] = acc[pl.ds(other, full), :].astype(send_ref.dtype)


def stage_kernel(scale, q_ref, g_ref, own_ref, q_out, g_out, own_out):
    q_out[...] = q_ref[...] * jnp.asarray(scale, q_ref.dtype)
    g_out[...] = g_ref[...]
    own_out[...] = own_ref[...]


def probs_kernel(reach, scale, place, first_ref, q_ref, g_ref, own_ref, *rest):
    mine_refs, other_refs, rest = rest[: reach // 2], rest[reach // 2 : reach], rest[reach:]
    p_ref, sum_ref, ext, down_ref, keep_ref, send_ref, s_buf, e_buf, peak_buf, acc, sem = rest
    step, steps = pl.program_id(0), pl.num_programs(0)
    rank, core = place[0], place[1]
    full = own_ref.shape[0]
    half = full // 2
    units = 2 * reach
    mask = lower_mask(half)
    far_bias = jnp.where(rank >= reach, 0.0, LOW).astype(jnp.float32)
    lowest = jnp.full((16, full), LOW, jnp.float32)

    def score(unit, rows, peak):
        block = unit_product(unit, ext, rows, half, reach, mask, far_bias)
        s_buf[unit * half : (unit + 1) * half] = block
        part = fold_rows(block, lowest, jnp.maximum)
        if unit >= 2:
            part = jnp.where(rank >= reach - unit // 2, part, LOW)
        return jnp.maximum(peak, part)

    def exponent(unit, level, total):
        at = slice(unit * half, (unit + 1) * half)
        if unit >= 2:
            level = jnp.where(rank >= reach - unit // 2, level, -LOW)
        expo = jnp.exp(s_buf[at] - level)
        e_buf[at] = expo
        return fold_rows(expo, total, jnp.add)

    def add_values(total):
        inv = 1.0 / jnp.sum(total, axis=0, keepdims=True)
        rounded = jnp.zeros((16, full), jnp.float32)
        for unit in range(units):
            at = slice(unit * half, (unit + 1) * half)
            tile = (e_buf[at] * inv).astype(jnp.bfloat16)
            p_ref[step, at] = tile
            rounded = fold_rows(tile.astype(jnp.float32), rounded, jnp.add)
            unit_add(unit, tile, acc, g_ref[...], half, reach, mask)
        rounded = jnp.sum(rounded, axis=0, keepdims=True)
        sum_ref[0] = jnp.broadcast_to(rounded, (8, full))

    @pl.when(step == 0)
    def _():
        copies = load_rows(own_ref, mine_refs, other_refs, ext, sem, core, full, reach)
        acc[...] = jnp.zeros_like(acc)
        for each in copies:
            each.wait()
        peak = lowest
        for unit in range(units):
            peak = score(unit, first_ref[...], peak)
        peak_buf[...] = peak

    @pl.when(step < steps - 1)
    def _():
        level = jnp.max(peak_buf[...], axis=0, keepdims=True)
        total = jnp.zeros((16, full), jnp.float32)
        peak = lowest
        for unit in range(units):
            total = exponent(unit, level, total)
            peak = score(unit, q_ref[...], peak)
        peak_buf[...] = peak
        add_values(total)

    @pl.when(step == steps - 1)
    def _():
        level = jnp.max(peak_buf[...], axis=0, keepdims=True)
        total = jnp.zeros((16, full), jnp.float32)
        for unit in range(units):
            total = exponent(unit, level, total)
        add_values(total)
        split_out(acc, down_ref, keep_ref, send_ref, core, full, reach)


def dscores_kernel(reach, scale, place, first_ref, q_ref, g_ref, first_sum, sum_ref, *rest):
    p_ref, own_ref, rest = rest[0], rest[1], rest[2:]
    mine_refs, other_refs, rest = rest[: reach // 2], rest[reach // 2 : reach], rest[reach:]
    ds_ref, down_ref, keep_ref, send_ref, ext, dp_buf, delta_buf, acc, sem = rest
    step, steps = pl.program_id(0), pl.num_programs(0)
    core = place[1]
    full = own_ref.shape[0]
    half = full // 2
    units = 2 * reach
    mask = lower_mask(half)

    def product(unit, grads, probs, total):
        at = slice(unit * half, (unit + 1) * half)
        block = unit_product(unit, ext, grads, half, reach, mask)
        dp_buf[at] = block
        return fold_rows(block * probs.astype(jnp.float32), total, jnp.add)

    def keep_delta(total, rounded):
        delta = jnp.sum(total, axis=0, keepdims=True) / rounded
        delta_buf[...] = jnp.broadcast_to(delta, delta_buf.shape)

    def dscore(unit, delta):
        at = slice(unit * half, (unit + 1) * half)
        tile = (p_ref[step, at].astype(jnp.float32) * (dp_buf[at] - delta)).astype(jnp.bfloat16)
        ds_ref[step, at] = tile
        return tile

    nothing = jnp.zeros((16, full), jnp.float32)

    @pl.when(step == 0)
    def _():
        copies = load_rows(own_ref, mine_refs, other_refs, ext, sem, core, full, reach)
        acc[...] = jnp.zeros_like(acc)
        for each in copies:
            each.wait()
        total = nothing
        for unit in range(units):
            tile = p_ref[0, unit * half : (unit + 1) * half]
            total = product(unit, first_ref[...], tile, total)
        keep_delta(total, first_sum[0, :1])

    @pl.when(step < steps - 1)
    def _():
        following = step + 1
        delta = delta_buf[:1]
        total = nothing
        for unit in range(units):
            unit_add(unit, dscore(unit, delta), acc, q_ref[...], half, reach, mask)
            tile = p_ref[following, unit * half : (unit + 1) * half]
            total = product(unit, g_ref[...], tile, total)
        keep_delta(total, sum_ref[0, :1])

    @pl.when(step == steps - 1)
    def _():
        delta = delta_buf[:1]
        for unit in range(units):
            unit_add(unit, dscore(unit, delta), acc, q_ref[...], half, reach, mask)
        split_out(acc, down_ref, keep_ref, send_ref, core, full, reach)


def dot_first(left, right):
    return lax.dot_general(
        left, right, (((0,), (0,)), ((), ())), preferred_element_type=jnp.float32
    )


def dquery_kernel(reach, scale, ds_ref, ext, dq_ref):
    full = ds_ref.shape[2]
    half = full // 2
    head = pl.program_id(0)
    mask = lower_mask(half)
    zero = jnp.zeros((half, half), jnp.bfloat16)
    own = reach * full
    lo_lo, lo_hi = ds_ref[head, :half, :half], ds_ref[head, :half, half:]
    hi_lo, hi_hi = ds_ref[head, half:full, :half], ds_ref[head, half:full, half:]
    lo = (
        dot_first(jnp.where(mask, lo_lo, zero), ext[own : own + half])
        + dot_first(jnp.where(mask, zero, lo_lo), ext[:half])
        + dot_first(hi_lo, ext[half:full])
    )
    hi = (
        dot_first(lo_hi, ext[own : own + half])
        + dot_first(jnp.where(mask, hi_hi, zero), ext[own + half : own + full])
        + dot_first(jnp.where(mask, zero, hi_hi), ext[half:full])
    )
    total = dot_first(ds_ref[head, full:own], ext[full:own])
    dq_ref[:half] = ((lo + total[:half]) * scale).astype(dq_ref.dtype)
    dq_ref[half:] = ((hi + total[half:]) * scale).astype(dq_ref.dtype)


def gather_halo(keys, values, reach, early):
    block, early = lax.optimization_barrier((along_seq(keys, 1, 1), early))
    mine = [block]
    for _ in range(1, reach // 2):
        mine.append(along_seq(mine[-1], 2, 0))
    last, value_block = lax.optimization_barrier((mine[-1], along_seq(values, 1, 1)))
    mine[-1] = last
    value_blocks = [value_block]
    for _ in range(1, reach // 2):
        value_blocks.append(along_seq(value_blocks[-1], 2, 0))
    return mine, [swap_heads(each, 1) for each in mine], value_blocks, early


def pair_sums(keep, send):
    return keep + swap_heads(send, 1).astype(jnp.float32)


def relay_back(parts, arrived):
    for j in range(len(parts) - 2, -1, -1):
        piece = (parts[j] + arrived.astype(jnp.float32)).astype(jnp.bfloat16)
        arrived = along_seq(piece, -2) if j else along_seq(piece, -1, -1)
    return arrived


def sum_chips(own):
    bit = 2
    while bit < lax.axis_size("head"):
        low = own.astype(jnp.bfloat16)
        own = low.astype(jnp.float32) + swap_heads(low, bit).astype(jnp.float32)
        bit *= 2
    return own


def own_half(down, low_core):
    half = down.shape[0] // 2
    mine = jnp.where(low_core, down[:half], down[half:])
    other = jnp.where(low_core, down[half:], down[:half])
    return mine + swap_heads(other.astype(jnp.bfloat16), 1).astype(jnp.float32)


def both_halves(own, low_core):
    other = swap_heads(own, 1)
    first_is_own = jnp.stack([low_core, jnp.logical_not(low_core)])[:, None, None]
    halves = jnp.where(first_is_own, own[None], other[None])
    return halves.reshape(2 * own.shape[0], own.shape[1])


def on_device(query, key_rows, value_rows, grad_out):
    tok_rows, head_dim = key_rows.shape
    heads = query.shape[1] // head_dim
    reach = WINDOW // tok_rows
    half = tok_rows // 2
    scale = head_dim ** (-0.5)
    core = lax.axis_index("head") % 2
    place = jnp.stack([lax.axis_index("seq"), core]).astype(jnp.int32)
    ext_rows = (reach + 1) * tok_rows
    span = reach * tok_rows

    def following(h):
        return jnp.minimum(h + 1, heads - 1)

    smem = pl.BlockSpec(memory_space=pltpu.SMEM)
    vmem = pl.BlockSpec(memory_space=pltpu.VMEM)
    halo = [pl.BlockSpec(memory_space=pl.ANY)] * (reach + 1)
    by_head = pl.BlockSpec((tok_rows, head_dim), lambda h: (0, h))
    by_head_next = pl.BlockSpec((tok_rows, head_dim), lambda h: (0, following(h)))
    by_head_first = pl.BlockSpec((tok_rows, head_dim), lambda h: (0, 0))
    row = pl.BlockSpec((1, 8, tok_rows), lambda h: (h, 0, 0))
    row_next = pl.BlockSpec((1, 8, tok_rows), lambda h: (following(h), 0, 0))
    row_first = pl.BlockSpec((1, 8, tok_rows), lambda h: (0, 0, 0))
    tile_shape = jax.ShapeDtypeStruct((heads, span, tok_rows), jnp.bfloat16)
    row_shape = jax.ShapeDtypeStruct((heads, 8, tok_rows), jnp.float32)

    down = pl.BlockSpec((tok_rows, head_dim), lambda h: (0, 0))
    whole = pl.BlockSpec((reach // 2, tok_rows, head_dim), lambda h: (0, 0, 0))
    sums = [down, whole, whole]
    sums_shapes = [
        jax.ShapeDtypeStruct((tok_rows, head_dim), jnp.float32),
        jax.ShapeDtypeStruct((reach // 2, tok_rows, head_dim), jnp.float32),
        jax.ShapeDtypeStruct((reach // 2, tok_rows, head_dim), jnp.bfloat16),
    ]
    ext = pltpu.VMEM((ext_rows, head_dim), jnp.bfloat16)
    acc = pltpu.VMEM((ext_rows, head_dim), jnp.float32)
    tile = pltpu.VMEM((span, tok_rows), jnp.float32)
    wide = pltpu.VMEM((16, tok_rows), jnp.float32)
    sems = pltpu.SemaphoreType.DMA((reach + 1,))
    product = 2 * heads * tok_rows * (reach * tok_rows + half) * head_dim

    def call(body, name, products, **spec):
        return pl.pallas_call(
            functools.partial(body, reach, scale),
            grid=(heads,),
            compiler_params=pltpu.CompilerParams(vmem_limit_bytes=VMEM_BYTES),
            cost_estimate=pl.CostEstimate(
                flops=products * product, bytes_accessed=16 * 2**20, transcendentals=0
            ),
            name=name,
            **spec,
        )

    staged = pl.pallas_call(
        functools.partial(stage_kernel, scale),
        out_shape=[
            jax.ShapeDtypeStruct(query.shape, query.dtype),
            jax.ShapeDtypeStruct(grad_out.shape, grad_out.dtype),
            jax.ShapeDtypeStruct(key_rows.shape, key_rows.dtype),
        ],
        in_specs=[vmem, vmem, vmem],
        out_specs=[vmem, vmem, vmem],
        compiler_params=pltpu.CompilerParams(vmem_limit_bytes=VMEM_BYTES),
        name="stage",
    )(query, grad_out, key_rows)
    early = (place, core == 0, staged)
    keys_mine, keys_other, values_mine, early = gather_halo(key_rows, value_rows, reach, early)
    place, low_core, (query_scaled, grads_own, keys_own) = early

    probs, rounded, keys_ext, dv_down, dv_keep, dv_send = call(
        probs_kernel,
        "probs",
        2,
        in_specs=[smem, by_head_first, by_head_next, by_head] + halo,
        out_specs=[vmem, row, vmem, *sums],
        out_shape=[
            tile_shape,
            row_shape,
            jax.ShapeDtypeStruct((ext_rows, head_dim), jnp.bfloat16),
            *sums_shapes,
        ],
        scratch_shapes=[tile, tile, wide, acc, sems],
    )(place, query_scaled, query_scaled, grads_own, keys_own, *keys_mine, *keys_other)

    values_mine, probs, dv_keep, dv_send = lax.optimization_barrier(
        (values_mine, probs, dv_keep, dv_send)
    )
    values_other = [swap_heads(block, 1) for block in values_mine]
    dv_parts = pair_sums(dv_keep, dv_send)
    dv_parts, probs = lax.optimization_barrier((dv_parts, probs))
    dv_back = along_seq(dv_parts[-1].astype(jnp.bfloat16), -2)

    dscores, dk_down, dk_keep, dk_send = call(
        dscores_kernel,
        "dscores",
        2,
        in_specs=[smem, by_head_first, by_head, by_head_next, row_first, row_next, vmem] + halo,
        out_specs=[vmem, *sums],
        out_shape=[tile_shape, *sums_shapes],
        scratch_shapes=[ext, tile, wide, acc, sems],
    )(
        place, grads_own, query_scaled, grads_own, rounded, rounded, probs, value_rows,
        *values_mine, *values_other,
    )

    dv_back, dk_keep, dk_send = lax.optimization_barrier((dv_back, dk_keep, dk_send))
    dk_parts = pair_sums(dk_keep, dk_send)
    dk_parts, dscores = lax.optimization_barrier((dk_parts, dscores))
    dk_back = along_seq(dk_parts[-1].astype(jnp.bfloat16), -2)
    dv_back = relay_back(dv_parts, dv_back)

    (grad_query,) = call(
        dquery_kernel,
        "dquery",
        1,
        in_specs=[vmem, vmem],
        out_specs=[by_head],
        out_shape=[jax.ShapeDtypeStruct(query.shape, query.dtype)],
    )(dscores, keys_ext)

    dk_back, dv_back, grad_query = lax.optimization_barrier((dk_back, dv_back, grad_query))
    dk_back = relay_back(dk_parts, dk_back)
    dv_own = sum_chips(dv_down + dv_back.astype(jnp.float32))
    dv_own, dk_back = lax.optimization_barrier((dv_own, dk_back))
    grad_value = dv_own + swap_heads(dv_own, 1)
    dk_own = own_half(dk_down + dk_back.astype(jnp.float32), low_core)
    grad_key = both_halves(sum_chips(dk_own), low_core)
    return grad_query, grad_key, grad_value


def solution(mesh):
    return jax.shard_map(
        on_device,
        mesh=mesh,
        in_specs=(P("seq", "head"), P("seq", None), P("seq", None), P("seq", "head")),
        out_specs=(P("seq", "head"), P("seq", None), P("seq", None)),
        check_vma=False,
    )
```

```python
import functools

import jax
import jax.numpy as jnp
from jax import lax
from jax.experimental import pallas as pl
from jax.experimental.pallas import tpu as pltpu
from jax.sharding import PartitionSpec as P

WINDOW = 2048
LOW = -1e30
VMEM_BYTES = 18 * 1024 * 1024


def along_seq(block, near, step=0, ring=True):
    shards, group = lax.axis_size("seq"), lax.axis_size("head")
    route = []
    for shard in range(shards):
        for member in range(group):
            target = shard + near + (member % 2) * step
            if ring or 0 <= target < shards:
                route.append((shard * group + member, target % shards * group + member))
    return lax.ppermute(block, ("seq", "head"), route)


def swap_heads(block, bit):
    route = [(i, i ^ bit) for i in range(lax.axis_size("head"))]
    return lax.ppermute(block, "head", route)


def dot_t(left, right):
    return lax.dot_general(
        left, right, (((1,), (1,)), ((), ())), preferred_element_type=jnp.float32
    )


def dot(left, right):
    return jnp.dot(left, right, preferred_element_type=jnp.float32)


def fold_rows(block, total, combine):
    rows = total.shape[0]
    for first in range(0, block.shape[0], rows):
        total = combine(total, block[first : first + rows])
    return total


def lower_mask(half):
    keys = lax.broadcasted_iota(jnp.int32, (half, half), 0)
    queries = lax.broadcasted_iota(jnp.int32, (half, half), 1)
    return queries >= keys


def load_rows(own_ref, mine_refs, other_refs, ext, sem, core, full, reach):
    copies = [pltpu.make_async_copy(own_ref, ext.at[pl.ds(reach * full, full)], sem.at[0])]
    for j in range(reach // 2):
        first = pl.multiple_of((reach - 1 - 2 * j - core) * full, full)
        other = pl.multiple_of((reach - 2 - 2 * j + core) * full, full)
        copies.append(
            pltpu.make_async_copy(mine_refs[j], ext.at[pl.ds(first, full)], sem.at[2 * j + 1])
        )
        copies.append(
            pltpu.make_async_copy(other_refs[j], ext.at[pl.ds(other, full)], sem.at[2 * j + 2])
        )
    for each in copies:
        each.start()
    return copies


def unit_product(unit, ext, rows, half, reach, mask, far_bias=None):
    own = reach * 2 * half
    if unit >= 2:
        return dot_t(ext[unit * half : (unit + 1) * half], rows)
    if unit == 0:
        near = dot_t(ext[own : own + half], rows)
        far = dot_t(ext[:half], rows[:half])
        if far_bias is not None:
            far = far + far_bias
        return jnp.concatenate([jnp.where(mask, near[:, :half], far), near[:, half:]], axis=1)
    near = dot_t(ext[own + half : own + 2 * half], rows[half:])
    far = dot_t(ext[half : 2 * half], rows)
    if far_bias is not None:
        far = far + far_bias
    return jnp.concatenate([far[:, :half], jnp.where(mask, near, far[:, half:])], axis=1)


def unit_add(unit, tile, acc, rows, half, reach, mask):
    own = reach * 2 * half
    if unit >= 2:
        acc[unit * half : (unit + 1) * half] += dot(tile, rows)
        return
    left, right = tile[:, :half], tile[:, half:]
    zero = jnp.zeros_like(left)
    if unit == 0:
        both = jnp.concatenate([jnp.where(mask, left, zero), right], axis=1)
        acc[own : own + half] += dot(both, rows)
        acc[:half] += dot(jnp.where(mask, zero, left), rows[:half])
        return
    acc[own + half : own + 2 * half] += dot(jnp.where(mask, right, zero), rows[half:])
    both = jnp.concatenate([left, jnp.where(mask, zero, right)], axis=1)
    acc[half : 2 * half] += dot(both, rows)


def split_out(acc, down_ref, keep_ref, send_ref, core, full, reach):
    down_ref[...] = acc[reach * full :]
    for j in range(reach // 2):
        first = pl.multiple_of((reach - 1 - 2 * j - core) * full, full)
        other = pl.multiple_of((reach - 2 - 2 * j + core) * full, full)
        keep_ref[j] = acc[pl.ds(first, full), :]
        send_ref[j] = acc[pl.ds(other, full), :].astype(send_ref.dtype)


def stage_kernel(scale, q_ref, g_ref, own_ref, q_out, g_out, own_out):
    q_out[...] = q_ref[...] * jnp.asarray(scale, q_ref.dtype)
    g_out[...] = g_ref[...]
    own_out[...] = own_ref[...]


def probs_kernel(reach, scale, place, first_ref, q_ref, g_ref, own_ref, *rest):
    mine_refs, other_refs, rest = rest[: reach // 2], rest[reach // 2 : reach], rest[reach:]
    p_ref, sum_ref, ext, down_ref, keep_ref, send_ref, s_buf, e_buf, peak_buf, acc, sem = rest
    step, steps = pl.program_id(0), pl.num_programs(0)
    rank, core = place[0], place[1]
    full = own_ref.shape[0]
    half = full // 2
    units = 2 * reach
    mask = lower_mask(half)
    far_bias = jnp.where(rank >= reach, 0.0, LOW).astype(jnp.float32)
    lowest = jnp.full((16, full), LOW, jnp.float32)

    def score(unit, rows, peak):
        block = unit_product(unit, ext, rows, half, reach, mask, far_bias)
        s_buf[unit * half : (unit + 1) * half] = block
        part = fold_rows(block, lowest, jnp.maximum)
        if unit >= 2:
            part = jnp.where(rank >= reach - unit // 2, part, LOW)
        return jnp.maximum(peak, part)

    def exponent(unit, level, total):
        at = slice(unit * half, (unit + 1) * half)
        if unit >= 2:
            level = jnp.where(rank >= reach - unit // 2, level, -LOW)
        expo = jnp.exp(s_buf[at] - level)
        e_buf[at] = expo
        return fold_rows(expo, total, jnp.add)

    def add_values(total):
        inv = 1.0 / jnp.sum(total, axis=0, keepdims=True)
        rounded = jnp.zeros((16, full), jnp.float32)
        for unit in range(units):
            at = slice(unit * half, (unit + 1) * half)
            tile = (e_buf[at] * inv).astype(jnp.bfloat16)
            p_ref[step, at] = tile
            rounded = fold_rows(tile.astype(jnp.float32), rounded, jnp.add)
            unit_add(unit, tile, acc, g_ref[...], half, reach, mask)
        rounded = jnp.sum(rounded, axis=0, keepdims=True)
        sum_ref[0] = jnp.broadcast_to(rounded, (8, full))

    @pl.when(step == 0)
    def _():
        copies = load_rows(own_ref, mine_refs, other_refs, ext, sem, core, full, reach)
        acc[...] = jnp.zeros_like(acc)
        for each in copies:
            each.wait()
        peak = lowest
        for unit in range(units):
            peak = score(unit, first_ref[...], peak)
        peak_buf[...] = peak

    @pl.when(step < steps - 1)
    def _():
        level = jnp.max(peak_buf[...], axis=0, keepdims=True)
        total = jnp.zeros((16, full), jnp.float32)
        peak = lowest
        for unit in range(units):
            total = exponent(unit, level, total)
            peak = score(unit, q_ref[...], peak)
        peak_buf[...] = peak
        add_values(total)

    @pl.when(step == steps - 1)
    def _():
        level = jnp.max(peak_buf[...], axis=0, keepdims=True)
        total = jnp.zeros((16, full), jnp.float32)
        for unit in range(units):
            total = exponent(unit, level, total)
        add_values(total)
        split_out(acc, down_ref, keep_ref, send_ref, core, full, reach)


def dscores_kernel(reach, scale, place, first_ref, q_ref, g_ref, first_sum, sum_ref, *rest):
    p_ref, own_ref, rest = rest[0], rest[1], rest[2:]
    mine_refs, other_refs, rest = rest[: reach // 2], rest[reach // 2 : reach], rest[reach:]
    ds_ref, down_ref, keep_ref, send_ref, ext, dp_buf, delta_buf, acc, sem = rest
    step, steps = pl.program_id(0), pl.num_programs(0)
    core = place[1]
    full = own_ref.shape[0]
    half = full // 2
    units = 2 * reach
    mask = lower_mask(half)

    def product(unit, grads, probs, total):
        at = slice(unit * half, (unit + 1) * half)
        block = unit_product(unit, ext, grads, half, reach, mask)
        dp_buf[at] = block
        return fold_rows(block * probs.astype(jnp.float32), total, jnp.add)

    def keep_delta(total, rounded):
        delta = jnp.sum(total, axis=0, keepdims=True) / rounded
        delta_buf[...] = jnp.broadcast_to(delta, delta_buf.shape)

    def dscore(unit, delta):
        at = slice(unit * half, (unit + 1) * half)
        tile = (p_ref[step, at].astype(jnp.float32) * (dp_buf[at] - delta)).astype(jnp.bfloat16)
        ds_ref[step, at] = tile
        return tile

    nothing = jnp.zeros((16, full), jnp.float32)

    @pl.when(step == 0)
    def _():
        copies = load_rows(own_ref, mine_refs, other_refs, ext, sem, core, full, reach)
        acc[...] = jnp.zeros_like(acc)
        for each in copies:
            each.wait()
        total = nothing
        for unit in range(units):
            tile = p_ref[0, unit * half : (unit + 1) * half]
            total = product(unit, first_ref[...], tile, total)
        keep_delta(total, first_sum[0, :1])

    @pl.when(step < steps - 1)
    def _():
        following = step + 1
        delta = delta_buf[:1]
        total = nothing
        for unit in range(units):
            unit_add(unit, dscore(unit, delta), acc, q_ref[...], half, reach, mask)
            tile = p_ref[following, unit * half : (unit + 1) * half]
            total = product(unit, g_ref[...], tile, total)
        keep_delta(total, sum_ref[0, :1])

    @pl.when(step == steps - 1)
    def _():
        delta = delta_buf[:1]
        for unit in range(units):
            unit_add(unit, dscore(unit, delta), acc, q_ref[...], half, reach, mask)
        split_out(acc, down_ref, keep_ref, send_ref, core, full, reach)


def dot_first(left, right):
    return lax.dot_general(
        left, right, (((0,), (0,)), ((), ())), preferred_element_type=jnp.float32
    )


def dquery_kernel(reach, scale, ds_ref, ext, dq_ref):
    full = ds_ref.shape[2]
    half = full // 2
    head = pl.program_id(0)
    mask = lower_mask(half)
    zero = jnp.zeros((half, half), jnp.bfloat16)
    own = reach * full
    lo_lo, lo_hi = ds_ref[head, :half, :half], ds_ref[head, :half, half:]
    hi_lo, hi_hi = ds_ref[head, half:full, :half], ds_ref[head, half:full, half:]
    lo = (
        dot_first(jnp.where(mask, lo_lo, zero), ext[own : own + half])
        + dot_first(jnp.where(mask, zero, lo_lo), ext[:half])
        + dot_first(hi_lo, ext[half:full])
    )
    hi = (
        dot_first(lo_hi, ext[own : own + half])
        + dot_first(jnp.where(mask, hi_hi, zero), ext[own + half : own + full])
        + dot_first(jnp.where(mask, zero, hi_hi), ext[half:full])
    )
    total = dot_first(ds_ref[head, full:own], ext[full:own])
    dq_ref[:half] = ((lo + total[:half]) * scale).astype(dq_ref.dtype)
    dq_ref[half:] = ((hi + total[half:]) * scale).astype(dq_ref.dtype)


def gather_halo(keys, values, reach, early):
    block, early = lax.optimization_barrier((along_seq(keys, 1, 1), early))
    mine = [block]
    for _ in range(1, reach // 2):
        mine.append(along_seq(mine[-1], 2, ring=False))
    last, value_block = lax.optimization_barrier((mine[-1], along_seq(values, 1, 1, ring=False)))
    mine[-1] = last
    value_blocks = [value_block]
    for _ in range(1, reach // 2):
        value_blocks.append(along_seq(value_blocks[-1], 2, 0))
    return mine, [swap_heads(each, 1) for each in mine], value_blocks, early


def pair_sums(keep, send):
    return keep + swap_heads(send, 1).astype(jnp.float32)


def relay_back(parts, arrived):
    for j in range(len(parts) - 2, -1, -1):
        piece = (parts[j] + arrived.astype(jnp.float32)).astype(jnp.bfloat16)
        arrived = along_seq(piece, -2) if j else along_seq(piece, -1, -1)
    return arrived


def sum_chips(own):
    bit = 2
    while bit < lax.axis_size("head"):
        low = own.astype(jnp.bfloat16)
        own = low.astype(jnp.float32) + swap_heads(low, bit).astype(jnp.float32)
        bit *= 2
    return own


def own_half(down, low_core):
    half = down.shape[0] // 2
    mine = jnp.where(low_core, down[:half], down[half:])
    other = jnp.where(low_core, down[half:], down[:half])
    return mine + swap_heads(other.astype(jnp.bfloat16), 1).astype(jnp.float32)


def both_halves(own, low_core):
    other = swap_heads(own, 1)
    first_is_own = jnp.stack([low_core, jnp.logical_not(low_core)])[:, None, None]
    halves = jnp.where(first_is_own, own[None], other[None])
    return halves.reshape(2 * own.shape[0], own.shape[1])


def on_device(query, key_rows, value_rows, grad_out):
    tok_rows, head_dim = key_rows.shape
    heads = query.shape[1] // head_dim
    reach = WINDOW // tok_rows
    half = tok_rows // 2
    scale = head_dim ** (-0.5)
    core = lax.axis_index("head") % 2
    place = jnp.stack([lax.axis_index("seq"), core]).astype(jnp.int32)
    ext_rows = (reach + 1) * tok_rows
    span = reach * tok_rows

    def following(h):
        return jnp.minimum(h + 1, heads - 1)

    smem = pl.BlockSpec(memory_space=pltpu.SMEM)
    vmem = pl.BlockSpec(memory_space=pltpu.VMEM)
    halo = [pl.BlockSpec(memory_space=pl.ANY)] * (reach + 1)
    by_head = pl.BlockSpec((tok_rows, head_dim), lambda h: (0, h))
    by_head_next = pl.BlockSpec((tok_rows, head_dim), lambda h: (0, following(h)))
    by_head_first = pl.BlockSpec((tok_rows, head_dim), lambda h: (0, 0))
    row = pl.BlockSpec((1, 8, tok_rows), lambda h: (h, 0, 0))
    row_next = pl.BlockSpec((1, 8, tok_rows), lambda h: (following(h), 0, 0))
    row_first = pl.BlockSpec((1, 8, tok_rows), lambda h: (0, 0, 0))
    tile_shape = jax.ShapeDtypeStruct((heads, span, tok_rows), jnp.bfloat16)
    row_shape = jax.ShapeDtypeStruct((heads, 8, tok_rows), jnp.float32)

    down = pl.BlockSpec((tok_rows, head_dim), lambda h: (0, 0))
    whole = pl.BlockSpec((reach // 2, tok_rows, head_dim), lambda h: (0, 0, 0))
    sums = [down, whole, whole]
    sums_shapes = [
        jax.ShapeDtypeStruct((tok_rows, head_dim), jnp.float32),
        jax.ShapeDtypeStruct((reach // 2, tok_rows, head_dim), jnp.float32),
        jax.ShapeDtypeStruct((reach // 2, tok_rows, head_dim), jnp.bfloat16),
    ]
    ext = pltpu.VMEM((ext_rows, head_dim), jnp.bfloat16)
    acc = pltpu.VMEM((ext_rows, head_dim), jnp.float32)
    tile = pltpu.VMEM((span, tok_rows), jnp.float32)
    wide = pltpu.VMEM((16, tok_rows), jnp.float32)
    sems = pltpu.SemaphoreType.DMA((reach + 1,))
    product = 2 * heads * tok_rows * (reach * tok_rows + half) * head_dim

    def call(body, name, products, **spec):
        return pl.pallas_call(
            functools.partial(body, reach, scale),
            grid=(heads,),
            compiler_params=pltpu.CompilerParams(vmem_limit_bytes=VMEM_BYTES),
            cost_estimate=pl.CostEstimate(
                flops=products * product, bytes_accessed=16 * 2**20, transcendentals=0
            ),
            name=name,
            **spec,
        )

    staged = pl.pallas_call(
        functools.partial(stage_kernel, scale),
        out_shape=[
            jax.ShapeDtypeStruct(query.shape, query.dtype),
            jax.ShapeDtypeStruct(grad_out.shape, grad_out.dtype),
            jax.ShapeDtypeStruct(key_rows.shape, key_rows.dtype),
        ],
        in_specs=[vmem, vmem, vmem],
        out_specs=[vmem, vmem, vmem],
        compiler_params=pltpu.CompilerParams(vmem_limit_bytes=VMEM_BYTES),
        name="stage",
    )(query, grad_out, key_rows)
    early = (place, core == 0, staged)
    keys_mine, keys_other, values_mine, early = gather_halo(key_rows, value_rows, reach, early)
    place, low_core, (query_scaled, grads_own, keys_own) = early

    probs, rounded, keys_ext, dv_down, dv_keep, dv_send = call(
        probs_kernel,
        "probs",
        2,
        in_specs=[smem, by_head_first, by_head_next, by_head] + halo,
        out_specs=[vmem, row, vmem, *sums],
        out_shape=[
            tile_shape,
            row_shape,
            jax.ShapeDtypeStruct((ext_rows, head_dim), jnp.bfloat16),
            *sums_shapes,
        ],
        scratch_shapes=[tile, tile, wide, acc, sems],
    )(place, query_scaled, query_scaled, grads_own, keys_own, *keys_mine, *keys_other)

    values_mine, probs, dv_keep, dv_send = lax.optimization_barrier(
        (values_mine, probs, dv_keep, dv_send)
    )
    values_other = [swap_heads(block, 1) for block in values_mine]
    dv_parts = pair_sums(dv_keep, dv_send)
    dv_parts, probs = lax.optimization_barrier((dv_parts, probs))
    dv_back = along_seq(dv_parts[-1].astype(jnp.bfloat16), -2, ring=False)

    dscores, dk_down, dk_keep, dk_send = call(
        dscores_kernel,
        "dscores",
        2,
        in_specs=[smem, by_head_first, by_head, by_head_next, row_first, row_next, vmem] + halo,
        out_specs=[vmem, *sums],
        out_shape=[tile_shape, *sums_shapes],
        scratch_shapes=[ext, tile, wide, acc, sems],
    )(
        place, grads_own, query_scaled, grads_own, rounded, rounded, probs, value_rows,
        *values_mine, *values_other,
    )

    dv_back, dk_keep, dk_send = lax.optimization_barrier((dv_back, dk_keep, dk_send))
    dk_parts = pair_sums(dk_keep, dk_send)
    dk_parts, dscores = lax.optimization_barrier((dk_parts, dscores))
    dk_back = along_seq(dk_parts[-1].astype(jnp.bfloat16), -2, ring=False)
    dv_back = relay_back(dv_parts, dv_back)

    (grad_query,) = call(
        dquery_kernel,
        "dquery",
        1,
        in_specs=[vmem, vmem],
        out_specs=[by_head],
        out_shape=[jax.ShapeDtypeStruct(query.shape, query.dtype)],
    )(dscores, keys_ext)

    dv_back, grad_query = lax.optimization_barrier((dv_back, grad_query))
    dk_back, grad_query = lax.optimization_barrier((dk_back, grad_query))
    dk_back = relay_back(dk_parts, dk_back)
    dv_own = sum_chips(dv_down + dv_back.astype(jnp.float32))
    dv_own, dk_back = lax.optimization_barrier((dv_own, dk_back))
    grad_value = dv_own + swap_heads(dv_own, 1)
    dk_own = own_half(dk_down + dk_back.astype(jnp.float32), low_core)
    grad_key = both_halves(sum_chips(dk_own), low_core)
    return grad_query, grad_key, grad_value


def solution(mesh):
    return jax.shard_map(
        on_device,
        mesh=mesh,
        in_specs=(P("seq", "head"), P("seq", None), P("seq", None), P("seq", "head")),
        out_specs=(P("seq", "head"), P("seq", None), P("seq", None)),
        check_vma=False,
    )
```
